32 devices in a mesh: blk: 8 (over z, y), rank: 4 (over x, core).
Axes of the slice: x: 2, y: 2, z: 4, core: 2. Of those that a mesh axis runs over, the one named last changes fastest.
Arguments:
- user_factors: float32 [256, 4096], P('rank', 'blk'), may hold values from -1.5 to 1.5
- item_factors: float32 [256, 8192], P('rank', 'blk'), may hold values from -1.5 to 1.5
- tile_rows: int32 [8, 4, 4096], P('blk'), may hold values from 0 to 511
- tile_cols: int32 [8, 4, 4096], P('blk'), may hold values from 0 to 1023
- tile_vals: float32 [8, 4, 4096], P('blk'), may hold values from -4 to 4
- tile_count: int32 [8, 4], P('blk'), may hold values from 512 to 4096, as said below
Outputs:
- new_users: float32 [256, 4096], P('rank', 'blk')
- new_items: float32 [256, 8192], P('rank', 'blk')
The draws below stay inside these ranges and needn't reach their ends.
Inputs may be any that keep to these rules, and one draw needn't show every extreme that they name: `tile_count`: in every stratum some block's tile is full (4096 live slots).
All inputs are finite; a program needn't handle non-finite values.
Results may differ from the reference program's by a relative error of at most 0.0003.
Values sent between devices are 32-bit elements; how exact they have to be, the bound alone decides.
A program may use at most 64 MiB of HBM per device.

```python
import jax
import jax.numpy as jnp
from jax import lax

R = 256
USERS_DEV = 512
ITEMS_DEV = 1024
TILE = 4096
BATCH = 1024
STRATA = 4
BLOCKS = 8
USERS = 4096
ITEMS = 8192


def draw_tile_count(key, part):
    key_counts, key_pick = jax.random.split(key)
    counts = jax.random.randint(key_counts, (BLOCKS, STRATA), TILE // 8, TILE + 1, dtype=jnp.int32)
    chosen = jax.random.randint(key_pick, (1, STRATA), 0, BLOCKS, dtype=jnp.int32)
    block_ids = jnp.arange(BLOCKS, dtype=jnp.int32)[:, None]
    return jnp.where(block_ids == chosen, TILE, counts).astype(jnp.int32)


def touch_ends(drawn, rng, low, top_value):
    dims = drawn.shape
    place = [jax.random.randint(jax.random.fold_in(rng, axis), (), 0, dims[axis]) for axis in range(len(dims))]
    drawn = drawn.at[tuple(place)].set(low)
    longest = dims.index(max(dims))
    place[longest] = (place[longest] + 1) % dims[longest]
    return drawn.at[tuple(place)].set(top_value)


def block_levels(own_key, extent, cuts, smallest, largest):
    gain, own = 1.0, jax.random.fold_in(own_key, 6)
    for axis_at, shards_of in cuts:
        heights = jnp.exp(jax.random.uniform(jax.random.fold_in(own, axis_at), (shards_of,), jnp.float32, smallest / len(cuts), largest / len(cuts)))
        gain = gain * jnp.repeat(heights, extent[axis_at] // shards_of).reshape([-1 if axis == axis_at else 1 for axis in range(len(extent))])
    return gain


def bell_draw(stream_key, extent, deviation, limit, cuts=(), kind=jnp.bfloat16):
    gain = block_levels(stream_key, extent, cuts, -0.22, 0.18) if cuts else 1.0
    values = jax.random.normal(stream_key, extent, jnp.float32) * deviation * gain
    return jnp.minimum(jnp.maximum(values, -limit), limit).astype(kind)


def setup_inputs(seed: int = 0) -> dict:
    key_list = jax.random.split(jax.random.key(seed), 7)
    return {
        "user_factors": bell_draw(key_list[0], (R, USERS), 0.25, 1.5, ((0, 4), (1, 8)), jnp.float32),
        "item_factors": bell_draw(key_list[1], (R, ITEMS), 0.25, 1.5, ((0, 4), (1, 8)), jnp.float32),
        "tile_rows": touch_ends(jax.random.randint(key_list[2], (BLOCKS, STRATA, TILE), 0, USERS_DEV), jax.random.fold_in(key_list[2], 1), 0, USERS_DEV - 1).astype(jnp.int32),
        "tile_cols": touch_ends(jax.random.randint(key_list[3], (BLOCKS, STRATA, TILE), 0, ITEMS_DEV), jax.random.fold_in(key_list[3], 1), 0, ITEMS_DEV - 1).astype(jnp.int32),
        "tile_vals": bell_draw(key_list[4], (BLOCKS, STRATA, TILE), 1.0, 4.0, ((0, 8),), jnp.float32),
        "tile_count": draw_tile_count(jax.random.fold_in(key_list[6], 71), 0),
    }


LEARN_RATE = 0.05
DECAY_WEIGHT = 0.02


def sweep_tile(user_block, item_block, row_index, col_index, rating_vals, live_count):
    def update(batch_index, carry):
        user_now, item_now = carry
        offset = (batch_index * BATCH).astype(jnp.int32)
        user_rows = lax.dynamic_slice_in_dim(row_index, offset, BATCH)
        item_rows = lax.dynamic_slice_in_dim(col_index, offset, BATCH)
        targets = lax.dynamic_slice_in_dim(rating_vals, offset, BATCH)
        positions = offset + jnp.arange(BATCH, dtype=jnp.int32)
        weights = (positions < live_count).astype(jnp.float32)
        user_vecs = user_now[user_rows]
        item_vecs = item_now[item_rows]
        predicted = jnp.sum(user_vecs * item_vecs, axis=1)
        errors = weights * (targets - predicted)
        user_step = LEARN_RATE * (errors[:, None] * item_vecs - DECAY_WEIGHT * weights[:, None] * user_vecs)
        item_step = LEARN_RATE * (errors[:, None] * user_vecs - DECAY_WEIGHT * weights[:, None] * item_vecs)
        return user_now.at[user_rows].add(user_step), item_now.at[item_rows].add(item_step)

    return lax.fori_loop(0, TILE // BATCH, update, (user_block, item_block))


def reference(user_factors, item_factors, tile_rows, tile_cols, tile_vals, tile_count):
    user_blocks = user_factors.T.reshape(BLOCKS, USERS_DEV, R)
    item_blocks = item_factors.T.reshape(BLOCKS, ITEMS_DEV, R)
    for stratum in range(STRATA):
        turned = jnp.roll(item_blocks, stratum, axis=0)
        user_blocks, turned = jax.vmap(sweep_tile)(user_blocks, turned, tile_rows[:, stratum], tile_cols[:, stratum], tile_vals[:, stratum], tile_count[:, stratum])
        item_blocks = jnp.roll(turned, -stratum, axis=0)
    return user_blocks.reshape(USERS, R).T, item_blocks.reshape(ITEMS, R).T
```

```python
import functools

import jax
import jax.numpy as jnp
from jax import lax
from jax.experimental import pallas as pl
from jax.experimental.pallas import tpu as pltpu
from jax.sharding import PartitionSpec as P

BATCH = 1024
LANES = 128
GROUPS = BATCH // LANES
CHUNK = 256
LEARN_RATE = 0.05
DECAY_WEIGHT = 0.02
MESH = pl.DeviceIdType.MESH


def split_rows(block):
    high = block.astype(jnp.bfloat16)
    low = (block - high.astype(jnp.float32)).astype(jnp.bfloat16)
    return high, low


def kernel(
    blocks, ranks,
    u_in, v_in, rows, cols, vals, count,
    u_out, v_out,
    users, u_cat, v_cat, held, tiles, chooser, u_pick, v_pick, u_step, v_step,
    partial, arrived, errs,
    part_send, part_recv, tile_send, tile_recv, user_send, user_recv,
):
    depth, user_count = u_in.shape
    item_count = v_in.shape[1]
    strata = rows.shape[1]
    tile = rows.shape[2]
    per_tile = tile // BATCH
    spans = tile // LANES
    batches = strata * per_tile
    blk = lax.axis_index("blk")
    rank = lax.axis_index("rank")

    def at_blk(shift):
        return (lax.rem(blk + (shift % blocks), blocks), rank)

    def at_rank(shift):
        return (blk, lax.rem(rank + (shift % ranks), ranks))

    barrier = pltpu.get_barrier_semaphore()
    met = [at_rank(o) for o in range(1, ranks)]
    met += [at_blk(o) for o in range(1, strata)] + [at_blk(-o) for o in range(1, strata)]
    for device in met:
        pl.semaphore_signal(barrier, inc=1, device_id=device, device_id_type=MESH)

    stratum_at = lax.broadcasted_iota(jnp.int32, (strata, LANES), 0)
    lane_at = lax.broadcasted_iota(jnp.int32, (strata, LANES), 1)
    live = jnp.zeros((strata, LANES), jnp.int32)
    for s in range(strata):
        live = jnp.where(stratum_at == s, count[0, s], live)
    for r in range(spans):
        here = slice(r * LANES, (r + 1) * LANES)
        alive = lane_at + r * LANES < live
        held[:, r, :] = jnp.where(alive, rows[0, :, here], -1).astype(jnp.float32)
        held[:, spans + r, :] = jnp.where(alive, cols[0, :, here], -1).astype(jnp.float32)
        held[:, 2 * spans + r, :] = vals[0, :, here]
    tiles[0] = held[0]

    def build(slot, s, q):
        at = pl.multiple_of(q * GROUPS, GROUPS)
        for base, size, first in ((0, user_count, 0), (user_count, item_count, spans)):
            index = tiles[s, pl.ds(first + at, GROUPS), :].astype(jnp.int32)
            for j in range(GROUPS):
                row = index[j : j + 1, :]
                for t in range(0, size, CHUNK):
                    place = lax.broadcasted_iota(jnp.int32, (CHUNK, LANES), 0) + t
                    chooser[slot, base + t : base + t + CHUNK, j * LANES : (j + 1) * LANES] = (
                        jnp.where(place == row, 1.0, 0.0).astype(jnp.bfloat16)
                    )

    def cut_users(s):
        high, low = split_rows(users[s])
        u_cat[:depth] = high
        u_cat[depth:] = low

    users[0] = u_in[...]
    v_out[...] = v_in[...]
    cut_users(0)
    high, low = split_rows(v_in[...])
    v_cat[:depth] = high
    v_cat[depth:] = low
    build(0, 0, 0)

    pl.semaphore_wait(barrier, len(met))

    def tile_copy(s):
        return pltpu.make_async_remote_copy(
            src_ref=held.at[s], dst_ref=tiles.at[s],
            send_sem=tile_send.at[s], recv_sem=tile_recv.at[s],
            device_id=(lax.rem(blk + blocks - s, blocks), rank),
            device_id_type=MESH,
        )

    for s in range(1, strata):
        tile_copy(s).start()

    def user_copy(s):
        return pltpu.make_async_remote_copy(
            src_ref=users.at[s], dst_ref=users.at[s + 1],
            send_sem=user_send.at[s], recv_sem=user_recv.at[s],
            device_id=at_blk(-1), device_id_type=MESH,
        )

    def part_copy(slot, o):
        return pltpu.make_async_remote_copy(
            src_ref=partial.at[slot], dst_ref=arrived.at[slot, o - 1],
            send_sem=part_send.at[slot, o - 1], recv_sem=part_recv.at[slot, o - 1],
            device_id=at_rank(o), device_id_type=MESH,
        )

    group_at = lax.broadcasted_iota(jnp.int32, (GROUPS, LANES), 0)

    @pl.loop(0, batches)
    def _(k):
        s = k // per_tile
        q = k % per_tile
        slot = k % 2
        total = jnp.zeros((GROUPS, LANES), jnp.float32)
        for c in range(0, BATCH, CHUNK):
            here = slice(c, c + CHUNK)
            u = jnp.dot(u_cat[...], chooser[slot, :user_count, here], preferred_element_type=jnp.float32)
            v = jnp.dot(v_cat[...], chooser[slot, user_count:, here], preferred_element_type=jnp.float32)
            u = u[:depth] + u[depth:]
            v = v[:depth] + v[depth:]
            u_pick[:, here] = u
            v_pick[:, here] = v
            sums = jnp.sum(u * v, axis=0, keepdims=True)
            for h in range(0, CHUNK, LANES):
                total = jnp.where(group_at == (c + h) // LANES, sums[:, h : h + LANES], total)
        partial[slot] = total
        for o in range(1, ranks):
            part_copy(slot, o).start()

        @pl.when(jnp.logical_and(q == per_tile - 1, s < strata - 1))
        def _():
            tile_copy(s + 1).wait_recv()

        @pl.when(k < batches - 1)
        def _():
            build((k + 1) % 2, (k + 1) // per_tile, (k + 1) % per_tile)

        for o in range(1, ranks):
            part_copy(slot, o).wait()
            total = total + arrived[slot, o - 1]
        at = pl.multiple_of(2 * spans + q * GROUPS, GROUPS)
        errs[...] = tiles[s, pl.ds(at, GROUPS), :] - total
        for j in range(GROUPS):
            here = slice(j * LANES, (j + 1) * LANES)
            e = errs[j : j + 1, :]
            u = u_pick[:, here]
            v = v_pick[:, here]
            high, low = split_rows(LEARN_RATE * (e * v - DECAY_WEIGHT * u))
            u_step[:depth, here] = high
            u_step[depth:, here] = low
            high, low = split_rows(LEARN_RATE * (e * u - DECAY_WEIGHT * v))
            v_step[:depth, here] = high
            v_step[depth:, here] = low

        def spread(steps, first):
            moved = lax.dot_general(
                steps[...], chooser[slot, first : first + CHUNK, :],
                (((1,), (1,)), ((), ())), preferred_element_type=jnp.float32,
            )
            return moved[:depth] + moved[depth:]

        for t in range(0, user_count, CHUNK):
            here = slice(t, t + CHUNK)
            new = users[s, :, here] + spread(u_step, t)
            users[s, :, here] = new
            high, low = split_rows(new)
            u_cat[:depth, here] = high
            u_cat[depth:, here] = low
        turn = jnp.logical_and(q == per_tile - 1, s < strata - 1)

        @pl.when(turn)
        def _():
            user_copy(s).start()

        for t in range(0, item_count, CHUNK):
            here = slice(t, t + CHUNK)
            new = v_out[:, here] + spread(v_step, user_count + t)
            v_out[:, here] = new
            high, low = split_rows(new)
            v_cat[:depth, here] = high
            v_cat[depth:, here] = low

        @pl.when(turn)
        def _():
            user_copy(s).wait()
            cut_users(s + 1)

    home = pltpu.make_async_remote_copy(
        src_ref=users.at[strata - 1], dst_ref=u_out,
        send_sem=user_send.at[strata - 1], recv_sem=user_recv.at[strata - 1],
        device_id=at_blk(strata - 1), device_id_type=MESH,
    )
    home.start()
    for s in range(1, strata):
        tile_copy(s).wait_send()
    home.wait()


def solution(mesh):
    blocks, ranks = mesh.shape["blk"], mesh.shape["rank"]

    def per_device(user_factors, item_factors, tile_rows, tile_cols, tile_vals, tile_count):
        depth, user_count = user_factors.shape
        item_count = item_factors.shape[1]
        strata, tile = tile_rows.shape[1:]
        held = (strata, 3 * tile // LANES, LANES)
        vmem = pl.BlockSpec(memory_space=pltpu.VMEM)
        f32, bf16 = jnp.float32, jnp.bfloat16
        return pl.pallas_call(
            functools.partial(kernel, blocks, ranks),
            out_shape=(
                jax.ShapeDtypeStruct((depth, user_count), f32),
                jax.ShapeDtypeStruct((depth, item_count), f32),
            ),
            in_specs=[vmem] * 5 + [pl.BlockSpec(memory_space=pltpu.SMEM)],
            out_specs=(vmem, vmem),
            scratch_shapes=[
                pltpu.VMEM((strata, depth, user_count), f32),
                pltpu.VMEM((2 * depth, user_count), bf16),
                pltpu.VMEM((2 * depth, item_count), bf16),
                pltpu.VMEM(held, f32),
                pltpu.VMEM(held, f32),
                pltpu.VMEM((2, user_count + item_count, BATCH), bf16),
                pltpu.VMEM((depth, BATCH), f32),
                pltpu.VMEM((depth, BATCH), f32),
                pltpu.VMEM((2 * depth, BATCH), bf16),
                pltpu.VMEM((2 * depth, BATCH), bf16),
                pltpu.VMEM((2, GROUPS, LANES), f32),
                pltpu.VMEM((2, ranks - 1, GROUPS, LANES), f32),
                pltpu.VMEM((GROUPS, LANES), f32),
                pltpu.SemaphoreType.DMA((2, ranks - 1)),
                pltpu.SemaphoreType.DMA((2, ranks - 1)),
                pltpu.SemaphoreType.DMA((strata,)),
                pltpu.SemaphoreType.DMA((strata,)),
                pltpu.SemaphoreType.DMA((strata,)),
                pltpu.SemaphoreType.DMA((strata,)),
            ],
            compiler_params=pltpu.CompilerParams(
                collective_id=0, has_side_effects=True, vmem_limit_bytes=32 * 1024 * 1024
            ),
        )(user_factors, item_factors, tile_rows, tile_cols, tile_vals, tile_count)

    placed = (
        P("rank", "blk"),
        P("rank", "blk"),
        P("blk", None, None),
        P("blk", None, None),
        P("blk", None, None),
        P("blk", None),
    )
    return jax.shard_map(
        per_device,
        mesh=mesh,
        in_specs=placed,
        out_specs=(P("rank", "blk"), P("rank", "blk")),
        check_vma=False,
    )
```

```python
import functools

import jax
import jax.numpy as jnp
from jax import lax
from jax.experimental import pallas as pl
from jax.experimental.pallas import tpu as pltpu
from jax.sharding import PartitionSpec as P

BATCH = 1024
LANES = 128
GROUPS = BATCH // LANES
CHUNK = 256
HALVES = 1
HALF = BATCH // HALVES
HALF_GROUPS = GROUPS // HALVES
LEARN_RATE = 0.05
DECAY_WEIGHT = 0.02
MESH = pl.DeviceIdType.MESH


def split_rows(block):
    high = block.astype(jnp.bfloat16)
    low = (block - high.astype(jnp.float32)).astype(jnp.bfloat16)
    return high, low


def kernel(
    blocks, ranks,
    u_in, v_in, rows_in, cols_in, vals_in, count_in,
    u_out, v_out,
    rows, cols, vals, count, users, u_cat, v_cat, held, tiles, chooser, spreader, u_pick, v_pick, u_step, v_step,
    partial, arrived, errs,
    part_send, part_recv, tile_send, tile_recv, user_send, user_recv, load_sem,
):
    depth, user_count = u_in.shape
    item_count = v_in.shape[1]
    strata, tile = rows_in.shape[1:]
    per_tile = tile // BATCH
    spans = tile // LANES
    batches = strata * per_tile
    blk = lax.axis_index("blk")
    rank = lax.axis_index("rank")

    def at_blk(shift):
        return (lax.rem(blk + (shift % blocks), blocks), rank)

    def at_rank(shift):
        return (blk, lax.rem(rank + (shift % ranks), ranks))

    barrier = pltpu.get_barrier_semaphore()
    met = [at_rank(o) for o in range(1, ranks)]
    met += [at_blk(o) for o in range(1, strata)] + [at_blk(-o) for o in range(1, strata)]
    for device in met:
        pl.semaphore_signal(barrier, inc=1, device_id=device, device_id_type=MESH)

    loads = [
        pltpu.make_async_copy(source, target, load_sem.at[i])
        for i, (source, target) in enumerate(
            (
                (count_in, count), (rows_in, rows), (cols_in, cols), (vals_in, vals),
                (u_in, users.at[0]), (v_in, v_out),
            )
        )
    ]
    for load in loads:
        load.start()
    for load in loads[:4]:
        load.wait()

    stratum_at = lax.broadcasted_iota(jnp.int32, (strata, LANES), 0)
    lane_at = lax.broadcasted_iota(jnp.int32, (strata, LANES), 1)
    live = jnp.zeros((strata, LANES), jnp.int32)
    for s in range(strata):
        live = jnp.where(stratum_at == s, count[0, s], live)
    for r in range(spans):
        here = slice(r * LANES, (r + 1) * LANES)
        alive = lane_at + r * LANES < live
        held[:, r, :] = jnp.where(alive, rows[0, :, here], -1).astype(jnp.float32)
        held[:, spans + r, :] = jnp.where(alive, cols[0, :, here], -1).astype(jnp.float32)
        held[:, 2 * spans + r, :] = vals[0, :, here]
    tiles[0] = held[0]

    parts = ((0, user_count, 0), (user_count, item_count, spans))
    down = lax.broadcasted_iota(jnp.int32, (CHUNK, LANES), 0)
    across = lax.broadcasted_iota(jnp.int32, (LANES, LANES), 1)

    def chosen(place, index):
        return jnp.where(place == index, 1.0, 0.0).astype(jnp.bfloat16)

    def index_of(s, q, first):
        at = pl.multiple_of(first + q * GROUPS, GROUPS)
        return tiles[s, pl.ds(at, GROUPS), :].astype(jnp.int32)

    def build_chooser(s, q):
        for base, size, first in parts:
            index = index_of(s, q, first)
            for j in range(GROUPS):
                row = jnp.broadcast_to(index[j : j + 1, :], (CHUNK, LANES))
                for t in range(0, size, CHUNK):
                    chooser[base + t : base + t + CHUNK, j * LANES : (j + 1) * LANES] = (
                        chosen(down + t, row)
                    )

    def build_spreader(s, q):
        for base, size, first in parts:
            index = jnp.transpose(index_of(s, q, first))
            for j in range(GROUPS):
                column = jnp.broadcast_to(index[:, j : j + 1], (LANES, LANES))
                for t in range(0, size, LANES):
                    spreader[j * LANES : (j + 1) * LANES, base + t : base + t + LANES] = (
                        chosen(across + t, column)
                    )

    def cut_users(s):
        high, low = split_rows(users[s])
        u_cat[:depth] = high
        u_cat[depth:] = low

    build_chooser(0, 0)
    for load in loads[4:]:
        load.wait()
    cut_users(0)
    high, low = split_rows(v_out[...])
    v_cat[:depth] = high
    v_cat[depth:] = low

    def tile_copy(s):
        return pltpu.make_async_remote_copy(
            src_ref=held.at[s], dst_ref=tiles.at[s],
            send_sem=tile_send.at[s], recv_sem=tile_recv.at[s],
            device_id=(lax.rem(blk + blocks - s, blocks), rank),
            device_id_type=MESH,
        )

    def user_copy(s):
        return pltpu.make_async_remote_copy(
            src_ref=users.at[s], dst_ref=users.at[s + 1],
            send_sem=user_send.at[s], recv_sem=user_recv.at[s],
            device_id=at_blk(-1), device_id_type=MESH,
        )

    def home():
        return pltpu.make_async_remote_copy(
            src_ref=users.at[strata - 1], dst_ref=u_out,
            send_sem=user_send.at[strata - 1], recv_sem=user_recv.at[strata - 1],
            device_id=at_blk(strata - 1), device_id_type=MESH,
        )

    def part_copy(slot, h, o):
        return pltpu.make_async_remote_copy(
            src_ref=partial.at[slot, h], dst_ref=arrived.at[slot, h, o - 1],
            send_sem=part_send.at[slot, h, o - 1], recv_sem=part_recv.at[slot, h, o - 1],
            device_id=at_rank(o), device_id_type=MESH,
        )

    group_at = lax.broadcasted_iota(jnp.int32, (HALF_GROUPS, LANES), 0)

    @pl.loop(0, batches)
    def _(k):
        s = k // per_tile
        q = k % per_tile
        slot = k % 2
        totals = []
        for h in range(HALVES):
            total = jnp.zeros((HALF_GROUPS, LANES), jnp.float32)
            for c in range(h * HALF, (h + 1) * HALF, CHUNK):
                here = slice(c, c + CHUNK)
                u = jnp.dot(u_cat[...], chooser[:user_count, here], preferred_element_type=jnp.float32)
                u = u[:depth] + u[depth:]
                v = jnp.dot(v_cat[...], chooser[user_count:, here], preferred_element_type=jnp.float32)
                v = v[:depth] + v[depth:]
                u_pick[:, here] = u
                v_pick[:, here] = v
                sums = jnp.sum(u * v, axis=0, keepdims=True)
                for g in range(0, CHUNK, LANES):
                    total = jnp.where(
                        group_at == (c - h * HALF + g) // LANES, sums[:, g : g + LANES], total
                    )
            partial[slot, h] = total
            if h == 0:

                @pl.when(k == 0)
                def _():
                    pl.semaphore_wait(barrier, len(met))

            for o in range(1, ranks):
                part_copy(slot, h, o).start()
            totals.append(total)
        turn = jnp.logical_and(q == per_tile - 1, s < strata - 1)

        @pl.when(k == 0)
        def _():
            for other in range(1, strata):
                tile_copy(other).start()

        build_spreader(s, q)

        @pl.when(turn)
        def _():
            tile_copy(s + 1).wait_recv()

        @pl.when(k < batches - 1)
        def _():
            build_chooser((k + 1) // per_tile, (k + 1) % per_tile)

        for h in range(HALVES):
            total = totals[h]
            for o in range(1, ranks):
                part_copy(slot, h, o).wait()
                total = total + arrived[slot, h, o - 1]
            at = pl.multiple_of(2 * spans + q * GROUPS, GROUPS)
            targets = tiles[s, pl.ds(at, GROUPS), :]
            errs[h] = targets[h * HALF_GROUPS : (h + 1) * HALF_GROUPS] - total
            for j in range(HALF_GROUPS):
                here = slice(h * HALF + j * LANES, h * HALF + (j + 1) * LANES)
                e = errs[h, j : j + 1, :]
                u = u_pick[:, here]
                v = v_pick[:, here]
                high, low = split_rows(LEARN_RATE * (e * v - DECAY_WEIGHT * u))
                u_step[:depth, here] = high
                u_step[depth:, here] = low
                high, low = split_rows(LEARN_RATE * (e * u - DECAY_WEIGHT * v))
                v_step[:depth, here] = high
                v_step[depth:, here] = low
            span = slice(h * HALF, (h + 1) * HALF)
            last = h == HALVES - 1

            def spread(steps, first):
                moved = jnp.dot(
                    steps[:, span], spreader[span, first : first + CHUNK],
                    preferred_element_type=jnp.float32,
                )
                return moved[:depth] + moved[depth:]

            for t in range(0, user_count, CHUNK):
                here = slice(t, t + CHUNK)
                new = users[s, :, here] + spread(u_step, t)
                users[s, :, here] = new
                if last:
                    high, low = split_rows(new)
                    u_cat[:depth, here] = high
                    u_cat[depth:, here] = low
            if last:

                @pl.when(turn)
                def _():
                    user_copy(s).start()

                @pl.when(k == batches - 1)
                def _():
                    home().start()

            for t in range(0, item_count, CHUNK):
                here = slice(t, t + CHUNK)
                new = v_out[:, here] + spread(v_step, user_count + t)
                v_out[:, here] = new
                if last:
                    high, low = split_rows(new)
                    v_cat[:depth, here] = high
                    v_cat[depth:, here] = low

        @pl.when(turn)
        def _():
            user_copy(s).wait()
            cut_users(s + 1)

    for s in range(1, strata):
        tile_copy(s).wait_send()
    home().wait()


def solution(mesh):
    blocks, ranks = mesh.shape["blk"], mesh.shape["rank"]

    def per_device(user_factors, item_factors, tile_rows, tile_cols, tile_vals, tile_count):
        depth, user_count = user_factors.shape
        item_count = item_factors.shape[1]
        strata, tile = tile_rows.shape[1:]
        held = (strata, 3 * tile // LANES, LANES)
        vmem = pl.BlockSpec(memory_space=pltpu.VMEM)
        f32, bf16 = jnp.float32, jnp.bfloat16
        return pl.pallas_call(
            functools.partial(kernel, blocks, ranks),
            out_shape=(
                jax.ShapeDtypeStruct((depth, user_count), f32),
                jax.ShapeDtypeStruct((depth, item_count), f32),
            ),
            in_specs=[pl.BlockSpec(memory_space=pl.ANY)] * 6,
            out_specs=(vmem, vmem),
            scratch_shapes=[
                pltpu.VMEM(tile_rows.shape, jnp.int32),
                pltpu.VMEM(tile_cols.shape, jnp.int32),
                pltpu.VMEM(tile_vals.shape, f32),
                pltpu.SMEM(tile_count.shape, jnp.int32),
                pltpu.VMEM((strata, depth, user_count), f32),
                pltpu.VMEM((2 * depth, user_count), bf16),
                pltpu.VMEM((2 * depth, item_count), bf16),
                pltpu.VMEM(held, f32),
                pltpu.VMEM(held, f32),
                pltpu.VMEM((user_count + item_count, BATCH), bf16),
                pltpu.VMEM((BATCH, user_count + item_count), bf16),
                pltpu.VMEM((depth, BATCH), f32),
                pltpu.VMEM((depth, BATCH), f32),
                pltpu.VMEM((2 * depth, BATCH), bf16),
                pltpu.VMEM((2 * depth, BATCH), bf16),
                pltpu.VMEM((2, HALVES, HALF_GROUPS, LANES), f32),
                pltpu.VMEM((2, HALVES, ranks - 1, HALF_GROUPS, LANES), f32),
                pltpu.VMEM((HALVES, HALF_GROUPS, LANES), f32),
                pltpu.SemaphoreType.DMA((2, HALVES, ranks - 1)),
                pltpu.SemaphoreType.DMA((2, HALVES, ranks - 1)),
                pltpu.SemaphoreType.DMA((strata,)),
                pltpu.SemaphoreType.DMA((strata,)),
                pltpu.SemaphoreType.DMA((strata,)),
                pltpu.SemaphoreType.DMA((strata,)),
                pltpu.SemaphoreType.DMA((6,)),
            ],
            compiler_params=pltpu.CompilerParams(
                collective_id=0, has_side_effects=True, vmem_limit_bytes=60 * 1024 * 1024
            ),
        )(user_factors, item_factors, tile_rows, tile_cols, tile_vals, tile_count)

    placed = (
        P("rank", "blk"),
        P("rank", "blk"),
        P("blk", None, None),
        P("blk", None, None),
        P("blk", None, None),
        P("blk", None),
    )
    return jax.shard_map(
        per_device,
        mesh=mesh,
        in_specs=placed,
        out_specs=(P("rank", "blk"), P("rank", "blk")),
        check_vma=False,
    )
```
